512 devices in a mesh: dp: 16 (over y, core), expert: 32 (over x, z).
Axes of the slice: x: 4, y: 8, z: 8, core: 2. Of those that a mesh axis runs over, the one named last changes fastest.
Arguments:
- tokens: bfloat16 [65536, 2048], P(('dp', 'expert')), may hold values from -6 to 6
- grad_out: bfloat16 [65536, 2048], P(('dp', 'expert')), may hold values from -3 to 3
- route_ids: int32 [65536, 2], P(('dp', 'expert')), may hold values from 0 to 31, all different within a row; in each aligned block of 128 rows (0 to 127, 128 to 255, ...) at most 10 rows name the same one
- route_probs: float32 [65536, 2], P(('dp', 'expert')), may hold values from 0.1 to 1
- gate_up: bfloat16 [32, 2, 2048, 768], P('expert', None, 'dp'), may hold values from -0.125 to 0.125
- w_down: bfloat16 [32, 768, 2048], P('expert', None, 'dp'), may hold values from -0.21875 to 0.21875
Outputs:
- input_grad: bfloat16 [65536, 2048], P(('dp', 'expert'))
- prob_grad: bfloat16 [65536, 2], P(('dp', 'expert'))
The draws below stay inside these ranges and needn't reach their ends.
Inputs may be any that keep to these rules, and one draw needn't show every extreme that they name: `route_ids`: within the rows of one device, no expert is named by more than 10 rows, and in every draw some device names some expert exactly 10 times; the 2 experts of a token differ.
All inputs are finite; a program needn't handle non-finite values.
Results may differ from the reference program's by a relative error of at most 0.0057.
Values may be sent and summed in bfloat16 or wider, within the bound.
No kernel may reach another device: no remote copies, remote signals or barrier semaphores. Data moves between devices by JAX's collectives and lax.ppermute only.
A program may use at most 64 MiB of HBM per device.

```python
import math
import jax
import jax.numpy as jnp
import numpy as np
from jax import lax

D = 2048
H = 768
TOPK = 2
TOK_DEV = 128
EXPERTS = 32
CAP = 10
TOKENS = 65536
N_DP = 16
N_EXPERT = 32


def block_scale(stream_key, dims, split, least, high):
    def one(axis_at, parts):
        draws = jax.random.uniform(jax.random.fold_in(jax.random.fold_in(stream_key, 6), axis_at), (parts,), jnp.float32, least / len(split), high / len(split))
        return jnp.repeat(jnp.exp(draws), dims[axis_at] // parts).reshape((-1,) + (1,) * (len(dims) - axis_at - 1))

    gain = one(*split[0])
    for cut in split[1:]:
        gain = gain * one(*cut)
    return gain


def assign_block(stream_key, own, number, rows, number_of, top, limit, lean):
    order = jax.random.permutation(stream_key, number_of)
    heavy_load, common = portions_of(number_of, rows * top, limit, lean, True), portions_of(number_of, rows * top, limit, lean, False)
    places = jnp.arange(number_of)

    def named(sizes, turn):
        used = int((sizes > 0).sum())
        fixed = max(1, used // 4)
        shifted = fixed + (places - fixed + turn * (used - fixed)) % max(1, number_of - fixed)
        return jnp.zeros((number_of,), jnp.int32).at[order[jnp.where(places < fixed, places, shifted)]].set(jnp.asarray(sizes, jnp.int32))

    sizes = jnp.where(number % 4 == 0, named(heavy_load, number // 4), named(common, number - number // 4 - 1))
    mixed = jax.random.permutation(jax.random.fold_in(own, 3), number_of)
    source_of, receiver = mixed[0:number_of // 2 * 2:2], mixed[1:number_of // 2 * 2:2]
    margin = jnp.minimum(sizes[source_of] - 1, limit - sizes[receiver]) // 2
    margin = jnp.where((source_of == order[0]) | (receiver == order[0]) | (sizes[receiver] == 0), 0, jnp.maximum(margin, 0))
    shifted = jax.random.randint(jax.random.fold_in(own, 4), (number_of // 2,), 0, 1 << 20) % (margin + 1)
    sizes = sizes.at[source_of].add(-shifted).at[receiver].add(shifted)
    labels = jnp.searchsorted(jnp.cumsum(sizes), jnp.arange(rows * top), side="right").astype(jnp.int32)
    table = labels.reshape(top, rows).T
    table = table[jax.random.permutation(jax.random.fold_in(own, 1), rows)]
    turn = jax.random.randint(jax.random.fold_in(own, 2), (rows, 1), 0, top)
    return jnp.take_along_axis(table, (jnp.arange(top)[None, :] + turn) % top, axis=1)


def portions_of(count, total, bound, lean, full):
    weights = [(1 << 20) // math.isqrt(grade ** lean) + 1 for grade in range(1, count + 1)]
    largest = bound if full else min(bound, max(-(-total // count), total * weights[0] // sum(weights)))
    least = 1 if total - largest >= count - 1 else 0
    given, surplus = [largest] + [least] * (count - 1), total - largest - least * (count - 1)
    while surplus > 0:
        free = [i for i in range(1, count) if given[i] < largest] or [i for i in range(1, count) if given[i] < bound]
        pool, remaining = sum([weights[i] for i in free]), surplus
        for i in free:
            extra = min(bound - given[i], max(1, remaining * weights[i] // pool), surplus)
            given[i] = given[i] + extra
            surplus = surplus - extra
    return np.array(given)


def gaussian(key, extent, deviation, bound, pieces=(), kind=jnp.bfloat16):
    array = deviation * jax.random.normal(key, extent, jnp.float32)
    if pieces:
        array = array * block_scale(key, extent, pieces, -0.22, 0.18)
    return jnp.clip(array, -bound, bound).astype(kind)


def setup_inputs(seed: int = 0) -> dict:
    splits = jax.random.split(jax.random.key(seed), 7)
    tokens = gaussian(splits[0], (TOKENS, D), 1.0, 6.0, ((0, 512),))
    grad_out = gaussian(splits[1], (TOKENS, D), 0.5, 3.0, ((0, 512),))
    route_ids_keys = jax.random.split(jax.random.fold_in(splits[2], 1), TOKENS // TOK_DEV)
    route_ids_turns = jax.random.permutation(jax.random.fold_in(splits[2], 3), TOKENS // TOK_DEV)
    route_ids = jax.vmap(lambda own, number: assign_block(jax.random.fold_in(splits[2], 2), own, number, TOK_DEV, EXPERTS, TOPK, CAP, 2))(route_ids_keys, route_ids_turns).reshape((TOKENS, TOPK))
    route_probs = jnp.clip(jnp.exp(math.log(1.0) - 2.3025851 * jax.random.uniform(splits[3], (TOKENS, TOPK), jnp.float32) ** block_scale(splits[3], (TOKENS, TOPK), ((0, 512),), -0.2, 0.2)), 0.1, 1.0)
    gate_up = gaussian(splits[4], (EXPERTS, 2, D, H), D ** -0.5, 0.125, ((0, 32), (2, 16)))
    w_down = gaussian(splits[5], (EXPERTS, H, D), H ** -0.5, 0.21875, ((0, 32), (2, 16)))
    return dict(tokens=tokens, grad_out=grad_out, route_ids=route_ids, route_probs=route_probs, gate_up=gate_up, w_down=w_down)


def expert_block(rows_in, rows_grad, gate_up, w_down):
    gate_pre = jnp.dot(rows_in, gate_up[0], preferred_element_type=jnp.float32)
    up_value = jnp.dot(rows_in, gate_up[1], preferred_element_type=jnp.float32)
    sigmoid_gate = jax.nn.sigmoid(gate_pre)
    activated = gate_pre * sigmoid_gate
    hidden = (activated * up_value).astype(jnp.bfloat16)
    expert_out = jnp.dot(hidden, w_down, preferred_element_type=jnp.float32)
    prob_grad = jnp.sum(rows_grad.astype(jnp.float32) * expert_out, axis=-1).astype(jnp.bfloat16)
    hidden_grad = jnp.dot(rows_grad, w_down.T, preferred_element_type=jnp.float32)
    gate_grad = (hidden_grad * up_value * sigmoid_gate * (1.0 + gate_pre * (1.0 - sigmoid_gate))).astype(jnp.bfloat16)
    up_grad = (hidden_grad * activated).astype(jnp.bfloat16)
    row_grad = jnp.dot(gate_grad, gate_up[0].T, preferred_element_type=jnp.float32)
    row_grad = row_grad + jnp.dot(up_grad, gate_up[1].T, preferred_element_type=jnp.float32)
    return row_grad.astype(jnp.bfloat16), prob_grad


def reference(tokens, grad_out, route_ids, route_probs, gate_up, w_down):
    pair_count = TOKENS * TOPK
    flat_ids = route_ids.reshape(-1).astype(jnp.int32)
    flat_probs = route_probs.reshape(-1)
    sorted_pairs = jnp.argsort(flat_ids, stable=True).astype(jnp.int32)
    counts = jax.ops.segment_sum(jnp.ones((pair_count,), jnp.int32), flat_ids, num_segments=EXPERTS)
    starts = (jnp.cumsum(counts) - counts).astype(jnp.int32)
    most_rows = N_DP * N_EXPERT * CAP
    padded = jnp.concatenate([sorted_pairs, jnp.zeros((most_rows,), jnp.int32)])

    def per_expert(state_pair, expert):
        grad_total, prob_total = state_pair
        picked = lax.dynamic_slice(padded, (starts[expert].astype(jnp.int32),), (most_rows,))
        filled = jnp.arange(most_rows, dtype=jnp.int32) < counts[expert]
        token_rows = (picked // TOPK).astype(jnp.int32)
        row_grad, prob_grad = expert_block(tokens[token_rows], grad_out[token_rows], gate_up[expert], w_down[expert])
        weight = flat_probs[picked]
        target = jnp.where(filled, token_rows, TOKENS).astype(jnp.int32)
        grad_total = grad_total.at[target].add(weight[:, None] * row_grad.astype(jnp.float32), mode="drop")
        pair_target = jnp.where(filled, picked, pair_count).astype(jnp.int32)
        prob_total = prob_total.at[pair_target].set(prob_grad, mode="drop")
        return (grad_total, prob_total), None

    initial = (jnp.zeros((TOKENS, D), jnp.float32), jnp.zeros((pair_count,), jnp.bfloat16))
    final, unused = lax.scan(per_expert, initial, jnp.arange(EXPERTS, dtype=jnp.int32))
    return final[0].astype(jnp.bfloat16), final[1].reshape(TOKENS, TOPK)
```

```python
import functools

import jax
import jax.numpy as jnp
from jax import lax
from jax.experimental import pallas as pl
from jax.experimental.pallas import tpu as pltpu
from jax.sharding import PartitionSpec as P

BF = jnp.bfloat16
F32 = jnp.float32
I32 = jnp.int32


def iota(shape, dim):
    return lax.broadcasted_iota(I32, shape, dim)


def row_quarter(j):
    return jnp.where(j < 32, j >> 3, (j - 32) >> 1)


def row_slot(j):
    return jnp.where(j < 32, j & 7, 8 + (j & 1))


def dot(a, b):
    return jnp.dot(a, b, preferred_element_type=F32)


def dot_nt(a, b):
    return lax.dot_general(a, b, (((1,), (1,)), ((), ())), preferred_element_type=F32)


def onehot(cond):
    return jnp.where(cond, 1.0, 0.0).astype(BF)


def ranks(ids, experts):
    toks = ids.shape[1]
    e = iota((experts, toks), 0)
    m0, m1 = e == ids[0:1, :], e == ids[1:2, :]
    o0, o1 = jnp.where(m0, 1.0, 0.0), jnp.where(m1, 1.0, 0.0)
    earlier = onehot(iota((toks, toks), 0) < iota((toks, toks), 1))
    r0 = dot(o0.astype(BF), earlier)
    r1 = dot(o1.astype(BF), earlier) + jnp.sum(o0, axis=1, keepdims=True)
    return jnp.where(m0, r0, -1.0), jnp.where(m1, r1, -1.0)


def weights_kernel(gu_ref, wd_ref, out_ref):
    out_ref[0:2] = gu_ref[0]
    eye = onehot(iota((128, 128), 0) == iota((128, 128), 1))
    out_ref[2] = dot_nt(eye, wd_ref[0]).astype(BF)


def pack_kernel(ids_ref, tok_ref, grad_ref, out_ref):
    experts = out_ref.shape[0]
    k0, k1 = ranks(ids_ref[...], experts)
    slot = jnp.maximum(k0, k1).astype(BF)
    quarters = lambda ref: jnp.concatenate([ref[:, q * 512 : (q + 1) * 512] for q in range(4)], axis=0)
    toks, grads = quarters(tok_ref), quarters(grad_ref)
    step = 8
    rows = step * 40
    row = iota((rows, 128), 0)
    j = row % 40
    want_slot = row_slot(j).astype(F32)
    want_q = row_quarter(j)
    local = iota((rows, experts), 0) // 40
    for b in range(experts // step):
        spread = onehot(local + b * step == iota((rows, experts), 1))
        hit = jnp.where(dot(spread, slot) == want_slot, 1.0, 0.0)
        pick = jnp.concatenate([jnp.where(want_q == q, hit, 0.0).astype(BF) for q in range(4)], axis=1)
        t = dot(pick, toks).reshape(step, 40, 512)
        g = dot(pick, grads).reshape(step, 40, 512)
        both = jnp.concatenate([t[:, :32], g[:, :32], t[:, 32:], g[:, 32:]], axis=1)
        out_ref[b * step : (b + 1) * step] = both.astype(BF)


def expert_kernel(x_ref, w_ref, out_ref, prob_ref, w, xs, gs, gg, ug, sems):
    sources = x_ref.shape[0]
    main, extra = sources * 8, sources * 2
    copies = [
        [
            pltpu.make_async_copy(
                w_ref.at[:, i, :, pl.ds(n * 256, 256)], w.at[i, :, :, pl.ds(n * 256, 256)], sems.at[n, i]
            )
            for i in range(3)
        ]
        for n in range(3)
    ]
    for group in copies:
        for c in group:
            c.start()
    tail = x_ref[:, 64:80, :].reshape(sources * 16, 512)
    src = iota((sources * 16, sources * 16), 1)
    dst = iota((sources * 16, sources * 16), 0)
    part, rest = dst // extra, dst % extra
    perm = onehot(src == (rest >> 1) * 16 + part * 2 + (rest & 1))
    tail = dot(perm, tail).astype(BF)
    for p in range(8):
        to = xs if p < 4 else gs
        cols = slice((p % 4) * 512, (p % 4 + 1) * 512)
        body = x_ref[:, p * 8 : (p + 1) * 8, :].astype(F32).reshape(main, 512)
        to[0:main, cols] = body.astype(BF)
        to[main : main + extra, cols] = tail[p * extra : (p + 1) * extra]
    prob = jnp.zeros((main + extra, 1), F32)
    for n in range(3):
        for c in copies[n]:
            c.wait()
        cols = slice(n * 256, (n + 1) * 256)
        gate_pre = dot(xs[...], w[0, :, :, cols].reshape(2048, 256))
        up_value = dot(xs[...], w[1, :, :, cols].reshape(2048, 256))
        hidden_grad = dot(gs[...], w[2, :, :, cols].reshape(2048, 256))
        sig = jax.nn.sigmoid(gate_pre)
        act = gate_pre * sig
        hidden = (act * up_value).astype(BF).astype(F32)
        prob = prob + jnp.sum(hidden * hidden_grad, axis=1, keepdims=True)
        gg[:, cols] = (hidden_grad * up_value * sig * (1.0 + gate_pre * (1.0 - sig))).astype(BF)
        ug[:, cols] = (hidden_grad * act).astype(BF)
    rows = main + extra
    row = iota((rows, 128), 0)
    lane = iota((rows, 128), 1)
    source = jnp.where(row < main, row >> 3, (row - main) >> 1)
    slot = jnp.where(row < main, row & 7, 8 + (row & 1))
    placed = jnp.where(lane == (source & 7) * 16 + slot, jnp.broadcast_to(prob, (rows, 128)), 0.0).astype(BF)
    row8 = iota((8, rows), 1)
    group = jnp.where(row8 < main, row8 >> 6, (row8 - main) >> 4)
    prob_ref[...] = dot(onehot(group == iota((8, rows), 0)), placed).astype(BF)
    tails = []
    for q in range(4):
        feats = slice(q * 4, (q + 1) * 4)
        row_grad = dot_nt(gg[...], w[0, feats].reshape(512, 768)) + dot_nt(ug[...], w[1, feats].reshape(512, 768))
        row_grad = row_grad.astype(BF)
        tails.append(row_grad[main:])
        xs[0:main, q * 512 : (q + 1) * 512] = row_grad[:main]
    tail = jnp.concatenate(tails, axis=0)
    dst = iota((4 * extra, 4 * extra), 0)
    src = iota((4 * extra, 4 * extra), 1)
    perm = onehot(src == ((dst >> 1) & 3) * extra + (dst >> 3) * 2 + (dst & 1))
    tail = dot(perm, tail).reshape(sources, 8, 512)
    body = [xs[0:main, q * 512 : (q + 1) * 512].astype(F32).reshape(sources, 8, 512) for q in range(4)]
    out_ref[...] = jnp.concatenate(body + [tail], axis=1).astype(BF)


def combine_kernel(ids_ref, ids_t_ref, p_ref, back_ref, prob_ref, out_ref, prob_out_ref):
    experts, per, width = back_ref.shape
    toks = p_ref.shape[0]
    k0, k1 = ranks(ids_ref[...], experts)
    for k, slots in enumerate((k0, k1)):
        acc = jnp.zeros((experts, toks), F32)
        for r in range(10):
            acc = acc + jnp.where(slots == r, jnp.broadcast_to(prob_ref[:, r : r + 1].astype(F32), (experts, toks)), 0.0)
        prob_out_ref[k : k + 1, :] = jnp.sum(acc, axis=0, keepdims=True).astype(BF)
    ids_t = ids_t_ref[...]
    e = iota((toks, experts), 1)
    m0, m1 = e == ids_t[:, 0:1], e == ids_t[:, 1:2]
    o0, o1 = jnp.where(m0, 1.0, 0.0), jnp.where(m1, 1.0, 0.0)
    earlier = onehot(iota((toks, toks), 1) < iota((toks, toks), 0))
    r0 = dot(earlier, o0.astype(BF))
    r1 = dot(earlier, o1.astype(BF)) + jnp.sum(o0, axis=0, keepdims=True)
    slot = jnp.concatenate([jnp.where(m0, r0, -1.0), jnp.where(m1, r1, -1.0)], axis=0).astype(BF)
    lanes = experts * per
    spread = onehot(iota((experts, lanes), 1) // per == iota((experts, lanes), 0))
    j = iota((1, lanes), 1) % per
    hit = jnp.where(dot(slot, spread) == row_slot(j).astype(F32), 1.0, 0.0)
    want_q = row_quarter(j)
    back = back_ref[...].astype(F32).reshape(lanes, width).astype(BF)
    p0, p1 = p_ref[:, 0:1], p_ref[:, 1:2]
    for q in range(4):
        rows = dot(jnp.where(want_q == q, hit, 0.0).astype(BF), back)
        out_ref[:, q * width : (q + 1) * width] = (p0 * rows[:toks] + p1 * rows[toks:]).astype(BF)


def params():
    return pltpu.CompilerParams(vmem_limit_bytes=56 * 1024 * 1024)


def cost(flops, size):
    return pl.CostEstimate(flops=flops, bytes_accessed=size, transcendentals=0)


def shards(tokens, grad_out, route_ids, route_probs, gate_up, w_down):
    toks, features = tokens.shape
    experts = lax.axis_size("expert")
    n_dp = lax.axis_size("dp")
    ids = route_ids.T
    own_w = pl.pallas_call(
        weights_kernel,
        out_shape=jax.ShapeDtypeStruct((3, 128, 768), BF),
        compiler_params=params(),
        cost_estimate=cost(10**8, 1200000),
        name="join_weights",
    )(gate_up, w_down)
    full_w = lax.all_gather(own_w, "dp", axis=0, tiled=False)
    send = pl.pallas_call(
        pack_kernel,
        out_shape=jax.ShapeDtypeStruct((experts, 80, 512), BF),
        compiler_params=params(),
        cost_estimate=cost(3 * 10**9, 4000000),
        name="pack_rows",
    )(ids, tokens, grad_out)
    rows = lax.all_to_all(send, "expert", split_axis=0, concat_axis=0, tiled=True)
    back, prob = pl.pallas_call(
        expert_kernel,
        in_specs=[pl.BlockSpec(memory_space=pltpu.VMEM), pl.BlockSpec(memory_space=pl.ANY)],
        out_shape=(jax.ShapeDtypeStruct((experts, 40, 512), BF), jax.ShapeDtypeStruct((8, 128), BF)),
        scratch_shapes=[
            pltpu.VMEM((3, n_dp, 128, 768), BF),
            pltpu.VMEM((experts * 10, features), BF),
            pltpu.VMEM((experts * 10, features), BF),
            pltpu.VMEM((experts * 10, 768), BF),
            pltpu.VMEM((experts * 10, 768), BF),
            pltpu.SemaphoreType.DMA((3, 3)),
        ],
        compiler_params=params(),
        cost_estimate=cost(6 * 10**9, 14000000),
        name="expert_rows",
    )(rows, full_w)
    probs = lax.all_gather(prob, "expert", axis=0, tiled=False)
    back = lax.all_to_all(back, "expert", split_axis=0, concat_axis=0, tiled=True)
    own = lax.axis_index("expert")
    own_prob = lax.dynamic_slice(probs, (0, own // 8, (own % 8) * 16), (experts, 1, 16))[:, 0]
    input_grad, prob_grad = pl.pallas_call(
        combine_kernel,
        out_shape=(jax.ShapeDtypeStruct((toks, features), BF), jax.ShapeDtypeStruct((2, toks), BF)),
        compiler_params=params(),
        cost_estimate=cost(2 * 10**9, 2000000),
        name="combine_rows",
    )(ids, route_ids, route_probs, back, own_prob)
    return input_grad, prob_grad.T


def solution(mesh):
    return jax.shard_map(
        shards,
        mesh=mesh,
        in_specs=(
            P(("dp", "expert"), None),
            P(("dp", "expert"), None),
            P(("dp", "expert"), None),
            P(("dp", "expert"), None),
            P("expert", None, "dp", None),
            P("expert", None, "dp"),
        ),
        out_specs=(P(("dp", "expert"), None), P(("dp", "expert"), None)),
        check_vma=False,
    )
```

```python
import jax
import jax.numpy as jnp
from jax import lax
from jax.experimental import pallas as pl
from jax.experimental.pallas import tpu as pltpu
from jax.sharding import PartitionSpec as P

BF = jnp.bfloat16
F32 = jnp.float32
I32 = jnp.int32


def iota(shape, dim):
    return lax.broadcasted_iota(I32, shape, dim)


def dot(a, b):
    return jnp.dot(a, b, preferred_element_type=F32)


def dot_nt(a, b):
    return lax.dot_general(a, b, (((1,), (1,)), ((), ())), preferred_element_type=F32)


def onehot(cond):
    return jnp.where(cond, 1.0, 0.0).astype(BF)


def ranks(ids, experts):
    toks = ids.shape[1]
    e = iota((experts, toks), 0)
    m0, m1 = e == ids[0:1, :], e == ids[1:2, :]
    o0, o1 = jnp.where(m0, 1.0, 0.0), jnp.where(m1, 1.0, 0.0)
    earlier = onehot(iota((toks, toks), 0) < iota((toks, toks), 1))
    r0 = dot(o0.astype(BF), earlier)
    r1 = dot(o1.astype(BF), earlier) + jnp.sum(o0, axis=1, keepdims=True)
    return jnp.where(m0, r0, -1.0), jnp.where(m1, r1, -1.0)


def weights_kernel(gu_ref, wd_ref, out_ref):
    out_ref[0:2] = gu_ref[0]
    eye = onehot(iota((128, 128), 0) == iota((128, 128), 1))
    out_ref[2] = dot_nt(eye, wd_ref[0]).astype(BF)


def quarters(x):
    return jnp.concatenate([x[:, q * 512 : (q + 1) * 512] for q in range(4)], axis=0)


def pack_kernel(ids_ref, tok_ref, grad_ref, out_ref):
    experts = out_ref.shape[0]
    toks = tok_ref.shape[0]
    k0, k1 = ranks(ids_ref[...], experts)
    slot = jnp.maximum(k0, k1).astype(BF)
    rows = experts * 8
    spread = onehot(iota((rows, experts), 0) >> 3 == iota((rows, experts), 1))
    ranked = dot(spread, slot)
    row = iota((rows, toks), 0)
    pick = onehot(ranked == (row & 7).astype(F32))
    late = jnp.where(ranked == (8 + (row & 1)).astype(F32), 1.0, 0.0)
    picks = jnp.concatenate([jnp.where((row & 7) >> 1 == q, late, 0.0).astype(BF) for q in range(4)], axis=1)
    refs = (tok_ref, grad_ref)
    for c in range(4):
        cols = slice(c * 512, (c + 1) * 512)
        parts = [dot(pick, ref[:, cols]).reshape(experts, 8, 512) for ref in refs]
        out_ref[:, :, cols] = jnp.concatenate(parts, axis=1).astype(BF)
    parts = [dot(picks, quarters(ref[...])).reshape(experts, 8, 512) for ref in refs]
    out_ref[:, :, 2048:2560] = jnp.concatenate(parts, axis=1).astype(BF)


def expert_kernel(x_ref, w_ref, out_ref, w, xs, gs, gg, ug, sems):
    sources = x_ref.shape[0]
    main, extra = sources * 8, sources * 2
    copies = [
        [
            pltpu.make_async_copy(
                w_ref.at[:, i, :, pl.ds(n * 256, 256)], w.at[i, :, :, pl.ds(n * 256, 256)], sems.at[n, i]
            )
            for i in range(3)
        ]
        for n in range(3)
    ]
    for group in copies:
        for c in group:
            c.start()
    for c in range(4):
        cols = slice(c * 512, (c + 1) * 512)
        both = x_ref[:, :, cols].astype(F32)
        xs[0:main, cols] = both[:, :8].reshape(main, 512).astype(BF)
        gs[0:main, cols] = both[:, 8:].reshape(main, 512).astype(BF)
    both = x_ref[:, :, 2048:2560].astype(F32)
    dst, src = iota((main, main), 0), iota((main, main), 1)
    gather = onehot(src == ((dst % extra) >> 1) * 8 + (dst // extra) * 2 + (dst & 1))
    for to, half in ((xs, both[:, :8]), (gs, both[:, 8:])):
        tail = dot(gather, half.reshape(main, 512).astype(BF)).astype(BF)
        for q in range(4):
            to[main : main + extra, q * 512 : (q + 1) * 512] = tail[q * extra : (q + 1) * extra]
    prob = jnp.zeros((main + extra, 1), F32)
    for n in range(3):
        for c in copies[n]:
            c.wait()
        cols = slice(n * 256, (n + 1) * 256)
        gate_pre = dot(xs[...], w[0, :, :, cols].reshape(2048, 256))
        up_value = dot(xs[...], w[1, :, :, cols].reshape(2048, 256))
        hidden_grad = dot(gs[...], w[2, :, :, cols].reshape(2048, 256))
        sig = jax.nn.sigmoid(gate_pre)
        act = gate_pre * sig
        hidden = (act * up_value).astype(BF).astype(F32)
        prob = prob + jnp.sum(hidden * hidden_grad, axis=1, keepdims=True)
        gg[:, cols] = (hidden_grad * up_value * sig * (1.0 + gate_pre * (1.0 - sig))).astype(BF)
        ug[:, cols] = (hidden_grad * act).astype(BF)
    rows = main + extra
    row, lane = iota((rows, 128), 0), iota((rows, 128), 1)
    slot = jnp.where(row < main, row & 7, 8 + (row & 1))
    placed = jnp.where(lane == slot, jnp.broadcast_to(prob, (rows, 128)), 0.0).astype(BF)
    at, row = iota((main, rows), 0), iota((main, rows), 1)
    source = jnp.where(row < main, row >> 3, (row - main) >> 1)
    placed = dot(onehot(at == source * 8), placed).reshape(sources, 8, 128)
    out_ref[:, :, 2560:2688] = placed.astype(BF)
    tails = []
    for q in range(4):
        feats = slice(q * 4, (q + 1) * 4)
        row_grad = dot_nt(gg[...], w[0, feats].reshape(512, 768)) + dot_nt(ug[...], w[1, feats].reshape(512, 768))
        tails.append(row_grad[main:].astype(BF))
        out_ref[:, :, q * 512 : (q + 1) * 512] = row_grad[:main].reshape(sources, 8, 512).astype(BF)
    tail = jnp.concatenate(tails, axis=0)
    scatter = onehot(src == ((dst >> 1) & 3) * extra + (dst >> 3) * 2 + (dst & 1))
    out_ref[:, :, 2048:2560] = dot(scatter, tail).reshape(sources, 8, 512).astype(BF)


def combine_kernel(ids_ref, ids_t_ref, p_ref, back_ref, out_ref, prob_out_ref):
    experts = back_ref.shape[0]
    toks = p_ref.shape[0]
    k0, k1 = ranks(ids_ref[...], experts)
    prob = back_ref[:, :, 2560:2688].astype(F32)[:, 0]
    for k, slots in enumerate((k0, k1)):
        acc = jnp.zeros((experts, toks), F32)
        for r in range(10):
            acc = acc + jnp.where(slots == r, jnp.broadcast_to(prob[:, r : r + 1], (experts, toks)), 0.0)
        prob_out_ref[k : k + 1, :] = jnp.sum(acc, axis=0, keepdims=True).astype(BF)
    ids_t = ids_t_ref[...]
    e = iota((toks, experts), 1)
    m0, m1 = e == ids_t[:, 0:1], e == ids_t[:, 1:2]
    o0, o1 = jnp.where(m0, 1.0, 0.0), jnp.where(m1, 1.0, 0.0)
    earlier = onehot(iota((toks, toks), 1) < iota((toks, toks), 0))
    r0 = dot(earlier, o0.astype(BF))
    r1 = dot(earlier, o1.astype(BF)) + jnp.sum(o0, axis=0, keepdims=True)
    slot = jnp.concatenate([jnp.where(m0, r0, -1.0), jnp.where(m1, r1, -1.0)], axis=0).astype(BF)
    lanes = experts * 8
    spread = onehot(iota((experts, lanes), 1) >> 3 == iota((experts, lanes), 0))
    ranked = dot(slot, spread)
    j = iota((2 * toks, lanes), 1) & 7
    pick = onehot(ranked == j.astype(F32))
    late = jnp.where(ranked == (8 + (j & 1)).astype(F32), 1.0, 0.0)
    tail = back_ref[:, :, 2048:2560].astype(F32).reshape(lanes, 512).astype(BF)
    p0, p1 = p_ref[:, 0:1], p_ref[:, 1:2]
    for q in range(4):
        cols = slice(q * 512, (q + 1) * 512)
        body = back_ref[:, :, cols].astype(F32).reshape(lanes, 512).astype(BF)
        rows = dot(pick, body) + dot(jnp.where(j >> 1 == q, late, 0.0).astype(BF), tail)
        out_ref[:, cols] = (p0 * rows[:toks] + p1 * rows[toks:]).astype(BF)


def params():
    return pltpu.CompilerParams(vmem_limit_bytes=56 * 1024 * 1024)


def cost(flops, size):
    return pl.CostEstimate(flops=flops, bytes_accessed=size, transcendentals=0)


def shards(tokens, grad_out, route_ids, route_probs, gate_up, w_down):
    toks, features = tokens.shape
    experts = lax.axis_size("expert")
    n_dp = lax.axis_size("dp")
    ids = route_ids.T
    own_w = pl.pallas_call(
        weights_kernel,
        out_shape=jax.ShapeDtypeStruct((3, 128, 768), BF),
        compiler_params=params(),
        cost_estimate=cost(10**8, 1200000),
        name="join_weights",
    )(gate_up, w_down)
    full_w = lax.all_gather(own_w, "dp", axis=0, tiled=False)
    send = pl.pallas_call(
        pack_kernel,
        out_shape=jax.ShapeDtypeStruct((experts, 16, 2560), BF),
        compiler_params=params(),
        cost_estimate=cost(3 * 10**9, 4000000),
        name="pack_rows",
    )(ids, tokens, grad_out)
    rows = lax.all_to_all(send, "expert", split_axis=0, concat_axis=0, tiled=True)
    back = pl.pallas_call(
        expert_kernel,
        in_specs=[pl.BlockSpec(memory_space=pltpu.VMEM), pl.BlockSpec(memory_space=pl.ANY)],
        out_shape=jax.ShapeDtypeStruct((experts, 8, 2688), BF),
        scratch_shapes=[
            pltpu.VMEM((3, n_dp, 128, 768), BF),
            pltpu.VMEM((experts * 10, features), BF),
            pltpu.VMEM((experts * 10, features), BF),
            pltpu.VMEM((experts * 10, 768), BF),
            pltpu.VMEM((experts * 10, 768), BF),
            pltpu.SemaphoreType.DMA((3, 3)),
        ],
        compiler_params=params(),
        cost_estimate=cost(6 * 10**9, 14000000),
        name="expert_rows",
    )(rows, full_w)
    back = lax.all_to_all(back, "expert", split_axis=0, concat_axis=0, tiled=True)
    input_grad, prob_grad = pl.pallas_call(
        combine_kernel,
        out_shape=(jax.ShapeDtypeStruct((toks, features), BF), jax.ShapeDtypeStruct((2, toks), BF)),
        compiler_params=params(),
        cost_estimate=cost(2 * 10**9, 2000000),
        name="combine_rows",
    )(ids, route_ids, route_probs, back)
    return input_grad, prob_grad.T


def solution(mesh):
    return jax.shard_map(
        shards,
        mesh=mesh,
        in_specs=(
            P(("dp", "expert"), None),
            P(("dp", "expert"), None),
            P(("dp", "expert"), None),
            P(("dp", "expert"), None),
            P("expert", None, "dp", None),
            P("expert", None, "dp"),
        ),
        out_specs=(P(("dp", "expert"), None), P(("dp", "expert"), None)),
        check_vma=False,
    )
```

```python
import jax
import jax.numpy as jnp
from jax import lax
from jax.experimental import pallas as pl
from jax.experimental.pallas import tpu as pltpu
from jax.sharding import PartitionSpec as P

BF = jnp.bfloat16
F32 = jnp.float32
I32 = jnp.int32


def iota(shape, dim):
    return lax.broadcasted_iota(I32, shape, dim)


def dot(a, b):
    return jnp.dot(a, b, preferred_element_type=F32)


def dot_nt(a, b):
    return lax.dot_general(a, b, (((1,), (1,)), ((), ())), preferred_element_type=F32)


def onehot(cond):
    return jnp.where(cond, 1.0, 0.0).astype(BF)


def ranks(ids, experts):
    toks = ids.shape[1]
    e = iota((experts, toks), 0)
    m0, m1 = e == ids[0:1, :], e == ids[1:2, :]
    o0, o1 = jnp.where(m0, 1.0, 0.0), jnp.where(m1, 1.0, 0.0)
    earlier = onehot(iota((toks, toks), 0) < iota((toks, toks), 1))
    r0 = dot(o0.astype(BF), earlier)
    r1 = dot(o1.astype(BF), earlier) + jnp.sum(o0, axis=1, keepdims=True)
    return jnp.where(m0, r0, -1.0), jnp.where(m1, r1, -1.0)


def weights_kernel(gu_ref, wd_ref, out_ref):
    out_ref[0:2] = gu_ref[0]
    eye = onehot(iota((128, 128), 0) == iota((128, 128), 1))
    out_ref[2] = dot_nt(eye, wd_ref[0]).astype(BF)


def quarters(x):
    return jnp.concatenate([x[:, q * 512 : (q + 1) * 512] for q in range(4)], axis=0)


def pack_kernel(ids_ref, tok_ref, grad_ref, out_ref):
    experts = out_ref.shape[0]
    toks = tok_ref.shape[0]
    k0, k1 = ranks(ids_ref[...], experts)
    slot = jnp.maximum(k0, k1).astype(BF)
    rows = experts * 8
    spread = onehot(iota((rows, experts), 0) >> 3 == iota((rows, experts), 1))
    ranked = dot(spread, slot)
    row = iota((rows, toks), 0)
    pick = onehot(ranked == (row & 7).astype(F32))
    late = jnp.where(ranked == (8 + (row & 1)).astype(F32), 1.0, 0.0)
    picks = jnp.concatenate([jnp.where((row & 7) >> 1 == q, late, 0.0).astype(BF) for q in range(4)], axis=1)
    refs = (tok_ref, grad_ref)
    for c in range(4):
        cols = slice(c * 512, (c + 1) * 512)
        parts = [dot(pick, ref[:, cols]).reshape(experts, 8, 512) for ref in refs]
        out_ref[:, :, cols] = jnp.concatenate(parts, axis=1).astype(BF)
    parts = [dot(picks, quarters(ref[...])).reshape(experts, 8, 512) for ref in refs]
    out_ref[:, :, 2048:2560] = jnp.concatenate(parts, axis=1).astype(BF)


def expert_kernel(x_ref, *refs):
    pieces, (out_ref, w, xs, gs, gg, ug, sems) = refs[:-7], refs[-7:]
    sources = x_ref.shape[0]
    main, extra = sources * 8, sources * 2
    me = lax.axis_index("dp")
    chips = w.shape[0] // 2
    chip, core = me // 2, me % 2
    places = []
    for hops in range(chips // 2 + 1):
        up, down = (chip + hops) % chips, (chip + chips - hops) % chips
        here = (down * (1 - core) + up * core) * 2
        there = (up * (1 - core) + down * core) * 2
        places += [here + core, here + 1 - core, there + 1 - core, there + core]
    places = places[:2] + places[4:-4] + [places[-4], places[-2]]
    blocks = list(zip(pieces, places, strict=True))
    copies = [
        [
            pltpu.make_async_copy(src.at[:, :, pl.ds(n * 256, 256)], w.at[at, :, :, pl.ds(n * 256, 256)], sems.at[n, i])
            for i, (src, at) in enumerate(blocks)
        ]
        for n in range(3)
    ]
    for group in copies:
        for c in group:
            c.start()
    for c in range(4):
        cols = slice(c * 512, (c + 1) * 512)
        both = x_ref[:, :, cols].astype(F32)
        xs[0:main, cols] = both[:, :8].reshape(main, 512).astype(BF)
        gs[0:main, cols] = both[:, 8:].reshape(main, 512).astype(BF)
    both = x_ref[:, :, 2048:2560].astype(F32)
    dst, src = iota((main, main), 0), iota((main, main), 1)
    gather = onehot(src == ((dst % extra) >> 1) * 8 + (dst // extra) * 2 + (dst & 1))
    for to, half in ((xs, both[:, :8]), (gs, both[:, 8:])):
        tail = dot(gather, half.reshape(main, 512).astype(BF)).astype(BF)
        for q in range(4):
            to[main : main + extra, q * 512 : (q + 1) * 512] = tail[q * extra : (q + 1) * extra]
    prob = jnp.zeros((main + extra, 1), F32)
    for n in range(3):
        for c in copies[n]:
            c.wait()
        cols = slice(n * 256, (n + 1) * 256)
        gate_pre = dot(xs[...], w[:, 0, :, cols].reshape(2048, 256))
        up_value = dot(xs[...], w[:, 1, :, cols].reshape(2048, 256))
        hidden_grad = dot(gs[...], w[:, 2, :, cols].reshape(2048, 256))
        sig = jax.nn.sigmoid(gate_pre)
        act = gate_pre * sig
        hidden = (act * up_value).astype(BF).astype(F32)
        prob = prob + jnp.sum(hidden * hidden_grad, axis=1, keepdims=True)
        gg[:, cols] = (hidden_grad * up_value * sig * (1.0 + gate_pre * (1.0 - sig))).astype(BF)
        ug[:, cols] = (hidden_grad * act).astype(BF)
    rows = main + extra
    row, lane = iota((rows, 128), 0), iota((rows, 128), 1)
    slot = jnp.where(row < main, row & 7, 8 + (row & 1))
    placed = jnp.where(lane == slot, jnp.broadcast_to(prob, (rows, 128)), 0.0).astype(BF)
    at, row = iota((main, rows), 0), iota((main, rows), 1)
    source = jnp.where(row < main, row >> 3, (row - main) >> 1)
    placed = dot(onehot(at == source * 8), placed).reshape(sources, 8, 128)
    out_ref[:, :, 2560:2688] = placed.astype(BF)
    tails = []
    for q in range(4):
        feats = slice(q * 4, (q + 1) * 4)
        row_grad = dot_nt(gg[...], w[feats, 0].reshape(512, 768)) + dot_nt(ug[...], w[feats, 1].reshape(512, 768))
        tails.append(row_grad[main:].astype(BF))
        out_ref[:, :, q * 512 : (q + 1) * 512] = row_grad[:main].reshape(sources, 8, 512).astype(BF)
    tail = jnp.concatenate(tails, axis=0)
    scatter = onehot(src == ((dst >> 1) & 3) * extra + (dst >> 3) * 2 + (dst & 1))
    out_ref[:, :, 2048:2560] = dot(scatter, tail).reshape(sources, 8, 512).astype(BF)


def combine_kernel(ids_ref, ids_t_ref, p_ref, back_ref, out_ref, prob_out_ref):
    experts = back_ref.shape[0]
    toks = p_ref.shape[0]
    k0, k1 = ranks(ids_ref[...], experts)
    prob = back_ref[:, :, 2560:2688].astype(F32)[:, 0]
    for k, slots in enumerate((k0, k1)):
        acc = jnp.zeros((experts, toks), F32)
        for r in range(10):
            acc = acc + jnp.where(slots == r, jnp.broadcast_to(prob[:, r : r + 1], (experts, toks)), 0.0)
        prob_out_ref[k : k + 1, :] = jnp.sum(acc, axis=0, keepdims=True).astype(BF)
    ids_t = ids_t_ref[...]
    e = iota((toks, experts), 1)
    m0, m1 = e == ids_t[:, 0:1], e == ids_t[:, 1:2]
    o0, o1 = jnp.where(m0, 1.0, 0.0), jnp.where(m1, 1.0, 0.0)
    earlier = onehot(iota((toks, toks), 1) < iota((toks, toks), 0))
    r0 = dot(earlier, o0.astype(BF))
    r1 = dot(earlier, o1.astype(BF)) + jnp.sum(o0, axis=0, keepdims=True)
    slot = jnp.concatenate([jnp.where(m0, r0, -1.0), jnp.where(m1, r1, -1.0)], axis=0).astype(BF)
    lanes = experts * 8
    spread = onehot(iota((experts, lanes), 1) >> 3 == iota((experts, lanes), 0))
    ranked = dot(slot, spread)
    j = iota((2 * toks, lanes), 1) & 7
    pick = onehot(ranked == j.astype(F32))
    late = jnp.where(ranked == (8 + (j & 1)).astype(F32), 1.0, 0.0)
    tail = back_ref[:, :, 2048:2560].astype(F32).reshape(lanes, 512).astype(BF)
    p0, p1 = p_ref[:, 0:1], p_ref[:, 1:2]
    for q in range(4):
        cols = slice(q * 512, (q + 1) * 512)
        body = back_ref[:, :, cols].astype(F32).reshape(lanes, 512).astype(BF)
        rows = dot(pick, body) + dot(jnp.where(j >> 1 == q, late, 0.0).astype(BF), tail)
        out_ref[:, cols] = (p0 * rows[:toks] + p1 * rows[toks:]).astype(BF)


def params():
    return pltpu.CompilerParams(vmem_limit_bytes=56 * 1024 * 1024)


def cost(flops, size):
    return pl.CostEstimate(flops=flops, bytes_accessed=size, transcendentals=0)


def ring(own, n_dp):
    swap = [(d, d ^ 1) for d in range(n_dp)]
    on = [(d, (d + 2 if d % 2 == 0 else d - 2) % n_dp) for d in range(n_dp)]
    pieces = [own, lax.ppermute(own, "dp", swap)]
    first, second = pieces
    for step in range(n_dp // 4 - 1):
        first, second = lax.ppermute(first, "dp", on), lax.ppermute(second, "dp", on)
        pieces += [first, second, lax.ppermute(first, "dp", swap), lax.ppermute(second, "dp", swap)]
    first = lax.ppermute(first, "dp", on)
    return pieces + [first, lax.ppermute(first, "dp", swap)]


def shards(tokens, grad_out, route_ids, route_probs, gate_up, w_down):
    toks, features = tokens.shape
    experts = lax.axis_size("expert")
    n_dp = lax.axis_size("dp")
    ids = route_ids.T
    send = pl.pallas_call(
        pack_kernel,
        out_shape=jax.ShapeDtypeStruct((experts, 16, 2560), BF),
        compiler_params=params(),
        cost_estimate=cost(10**9, 4000000),
        name="pack_rows",
    )(ids, tokens, grad_out)
    rows = lax.all_to_all(send, "expert", split_axis=0, concat_axis=0, tiled=True)
    own_w = pl.pallas_call(
        weights_kernel,
        out_shape=jax.ShapeDtypeStruct((3, 128, 768), BF),
        compiler_params=params(),
        cost_estimate=cost(10**8, 1200000),
        name="join_weights",
    )(gate_up, w_down)
    pieces = ring(own_w, n_dp)
    back = pl.pallas_call(
        expert_kernel,
        in_specs=[pl.BlockSpec(memory_space=pltpu.VMEM)] + [pl.BlockSpec(memory_space=pl.ANY)] * len(pieces),
        out_shape=jax.ShapeDtypeStruct((experts, 8, 2688), BF),
        scratch_shapes=[
            pltpu.VMEM((n_dp, 3, 128, 768), BF),
            pltpu.VMEM((experts * 10, features), BF),
            pltpu.VMEM((experts * 10, features), BF),
            pltpu.VMEM((experts * 10, 768), BF),
            pltpu.VMEM((experts * 10, 768), BF),
            pltpu.SemaphoreType.DMA((3, n_dp)),
        ],
        compiler_params=params(),
        cost_estimate=cost(6 * 10**9, 14000000),
        name="expert_rows",
    )(rows, *pieces)
    back = lax.all_to_all(back, "expert", split_axis=0, concat_axis=0, tiled=True)
    input_grad, prob_grad = pl.pallas_call(
        combine_kernel,
        out_shape=(jax.ShapeDtypeStruct((toks, features), BF), jax.ShapeDtypeStruct((2, toks), BF)),
        compiler_params=params(),
        cost_estimate=cost(2 * 10**9, 2000000),
        name="combine_rows",
    )(ids, route_ids, route_probs, back)
    return input_grad, prob_grad.T


def solution(mesh):
    return jax.shard_map(
        shards,
        mesh=mesh,
        in_specs=(
            P(("dp", "expert"), None),
            P(("dp", "expert"), None),
            P(("dp", "expert"), None),
            P(("dp", "expert"), None),
            P("expert", None, "dp", None),
            P("expert", None, "dp"),
        ),
        out_specs=(P(("dp", "expert"), None), P(("dp", "expert"), None)),
        check_vma=False,
    )
```

```python
import jax
import jax.numpy as jnp
from jax import lax
from jax.experimental import pallas as pl
from jax.experimental.pallas import tpu as pltpu
from jax.sharding import PartitionSpec as P

BF = jnp.bfloat16
F32 = jnp.float32
I32 = jnp.int32


def iota(shape, dim):
    return lax.broadcasted_iota(I32, shape, dim)


def dot(a, b):
    return jnp.dot(a, b, preferred_element_type=F32)


def dot_nt(a, b):
    return lax.dot_general(a, b, (((1,), (1,)), ((), ())), preferred_element_type=F32)


def onehot(cond):
    return jnp.where(cond, 1.0, 0.0).astype(BF)


def ranks(ids, experts):
    toks = ids.shape[1]
    e = iota((experts, toks), 0)
    m0, m1 = e == ids[0:1, :], e == ids[1:2, :]
    o0, o1 = jnp.where(m0, 1.0, 0.0), jnp.where(m1, 1.0, 0.0)
    earlier = onehot(iota((toks, toks), 0) < iota((toks, toks), 1))
    r0 = dot(o0.astype(BF), earlier)
    r1 = dot(o1.astype(BF), earlier) + jnp.sum(o0, axis=1, keepdims=True)
    return jnp.where(m0, r0, -1.0), jnp.where(m1, r1, -1.0)


def weights_kernel(gu_ref, wd_ref, out_ref):
    out_ref[0:2] = gu_ref[0]
    eye = onehot(iota((128, 128), 0) == iota((128, 128), 1))
    out_ref[2] = dot_nt(eye, wd_ref[0]).astype(BF)


def quarters(x):
    return jnp.concatenate([x[:, q * 512 : (q + 1) * 512] for q in range(4)], axis=0)


def stream(src, dst, sems, columns):
    return [
        pltpu.make_async_copy(src.at[:, :, pl.ds(at, size)], dst.at[:, :, pl.ds(at, size)], sems.at[i])
        for i, (at, size) in enumerate(columns)
    ]


def pack_kernel(ids_hbm, tok_hbm, grad_hbm, out_hbm, ids_ref, tok_ref, grad_ref, out_ref, sems, out_sems):
    refs = (tok_ref, grad_ref)
    ids_load = pltpu.make_async_copy(ids_hbm, ids_ref, sems.at[2])
    ids_load.start()
    loads = [pltpu.make_async_copy(src, to, sems.at[i]) for i, (src, to) in enumerate(zip((tok_hbm, grad_hbm), refs))]
    for load in loads:
        load.start()
    experts = out_ref.shape[0]
    toks = tok_ref.shape[0]
    ids_load.wait()
    k0, k1 = ranks(ids_ref[...], experts)
    slot = jnp.maximum(k0, k1).astype(BF)
    rows = experts * 8
    spread = onehot(iota((rows, experts), 0) >> 3 == iota((rows, experts), 1))
    ranked = dot(spread, slot)
    row = iota((rows, toks), 0)
    pick = onehot(ranked == (row & 7).astype(F32))
    late = jnp.where(ranked == (8 + (row & 1)).astype(F32), 1.0, 0.0)
    picks = jnp.concatenate([jnp.where((row & 7) >> 1 == q, late, 0.0).astype(BF) for q in range(4)], axis=1)
    for load in loads:
        load.wait()
    stores = stream(out_ref, out_hbm, out_sems, [(c * 512, 512) for c in range(5)])
    for c in range(4):
        cols = slice(c * 512, (c + 1) * 512)
        parts = [dot(pick, ref[:, cols]).reshape(experts, 8, 512) for ref in refs]
        out_ref[:, :, cols] = jnp.concatenate(parts, axis=1).astype(BF)
        stores[c].start()
    parts = [dot(picks, quarters(ref[...])).reshape(experts, 8, 512) for ref in refs]
    out_ref[:, :, 2048:2560] = jnp.concatenate(parts, axis=1).astype(BF)
    stores[4].start()
    for store in stores:
        store.wait()


def owners(dp, n_dp):
    chips, chip, core = n_dp // 2, dp >> 1, dp & 1
    out = []
    for hops in range(chips // 2 + 1):
        up, down = (chip + hops) % chips, (chip + chips - hops) % chips
        here = (down * (1 - core) + up * core) * 2
        there = (up * (1 - core) + down * core) * 2
        out += [here + core, here + 1 - core, there + 1 - core, there + core]
    return out[:2] + out[4:-4] + [out[-4], out[-2]]


def expert_kernel(x_hbm, *refs):
    pieces, (out_hbm, x_ref, w, xs, gs, gg, ug, out_ref, x_sems, sems, out_sems) = refs[:-11], refs[-11:]
    sources = x_ref.shape[0]
    main, extra = sources * 8, sources * 2
    places = owners(lax.axis_index("dp"), len(pieces))
    loads = stream(x_hbm, x_ref, x_sems, [(c * 512, 512) for c in range(5)])
    for load in loads:
        load.start()
    copies = []
    for n in range(3):
        cols = pl.ds(n * 256, 256)
        copies.append(
            [
                pltpu.make_async_copy(src.at[:, :, cols], w.at[at, :, :, cols], sems.at[n, i])
                for i, (src, at) in enumerate(zip(pieces, places, strict=True))
            ]
        )
    for c in copies[0]:
        c.start()
    stores = stream(out_ref, out_hbm, out_sems, [(q * 512, 512) for q in range(5)] + [(2560, 128)])
    for c in range(4):
        loads[c].wait()
        cols = slice(c * 512, (c + 1) * 512)
        both = x_ref[:, :, cols].astype(F32)
        xs[0:main, cols] = both[:, :8].reshape(main, 512).astype(BF)
        gs[0:main, cols] = both[:, 8:].reshape(main, 512).astype(BF)
    for c in copies[1]:
        c.start()
    loads[4].wait()
    both = x_ref[:, :, 2048:2560].astype(F32)
    dst, src = iota((main, main), 0), iota((main, main), 1)
    gather = onehot(src == ((dst % extra) >> 1) * 8 + (dst // extra) * 2 + (dst & 1))
    for to, half in ((xs, both[:, :8]), (gs, both[:, 8:])):
        tail = dot(gather, half.reshape(main, 512).astype(BF)).astype(BF)
        for q in range(4):
            to[main : main + extra, q * 512 : (q + 1) * 512] = tail[q * extra : (q + 1) * extra]
    prob = jnp.zeros((main + extra, 1), F32)
    for n in range(3):
        for c in copies[n]:
            c.wait()
        if n == 0:
            for c in copies[2]:
                c.start()
        cols = slice(n * 256, (n + 1) * 256)
        gate_pre = dot(xs[...], w[:, 0, :, cols].reshape(2048, 256))
        up_value = dot(xs[...], w[:, 1, :, cols].reshape(2048, 256))
        hidden_grad = dot(gs[...], w[:, 2, :, cols].reshape(2048, 256))
        sig = jax.nn.sigmoid(gate_pre)
        act = gate_pre * sig
        hidden = (act * up_value).astype(BF).astype(F32)
        prob = prob + jnp.sum(hidden * hidden_grad, axis=1, keepdims=True)
        gg[:, cols] = (hidden_grad * up_value * sig * (1.0 + gate_pre * (1.0 - sig))).astype(BF)
        ug[:, cols] = (hidden_grad * act).astype(BF)
    rows = main + extra
    row, lane = iota((rows, 128), 0), iota((rows, 128), 1)
    slot = jnp.where(row < main, row & 7, 8 + (row & 1))
    placed = jnp.where(lane == slot, jnp.broadcast_to(prob, (rows, 128)), 0.0).astype(BF)
    at, row = iota((main, rows), 0), iota((main, rows), 1)
    source = jnp.where(row < main, row >> 3, (row - main) >> 1)
    placed = dot(onehot(at == source * 8), placed).reshape(sources, 8, 128)
    out_ref[:, :, 2560:2688] = placed.astype(BF)
    stores[5].start()
    tails = []
    for q in range(4):
        feats = slice(q * 4, (q + 1) * 4)
        row_grad = dot_nt(gg[...], w[feats, 0].reshape(512, 768)) + dot_nt(ug[...], w[feats, 1].reshape(512, 768))
        tails.append(row_grad[main:].astype(BF))
        out_ref[:, :, q * 512 : (q + 1) * 512] = row_grad[:main].reshape(sources, 8, 512).astype(BF)
        stores[q].start()
    tail = jnp.concatenate(tails, axis=0)
    scatter = onehot(src == ((dst >> 1) & 3) * extra + (dst >> 3) * 2 + (dst & 1))
    out_ref[:, :, 2048:2560] = dot(scatter, tail).reshape(sources, 8, 512).astype(BF)
    stores[4].start()
    for store in stores:
        store.wait()


def combine_kernel(ids_ref, ids_t_ref, p_ref, back_ref, out_ref, prob_out_ref):
    experts = back_ref.shape[0]
    toks = p_ref.shape[0]
    k0, k1 = ranks(ids_ref[...], experts)
    prob = back_ref[:, :, 2560:2688].astype(F32)[:, 0]
    for k, slots in enumerate((k0, k1)):
        acc = jnp.zeros((experts, toks), F32)
        for r in range(10):
            acc = acc + jnp.where(slots == r, jnp.broadcast_to(prob[:, r : r + 1], (experts, toks)), 0.0)
        prob_out_ref[k : k + 1, :] = jnp.sum(acc, axis=0, keepdims=True).astype(BF)
    ids_t = ids_t_ref[...]
    e = iota((toks, experts), 1)
    m0, m1 = e == ids_t[:, 0:1], e == ids_t[:, 1:2]
    o0, o1 = jnp.where(m0, 1.0, 0.0), jnp.where(m1, 1.0, 0.0)
    earlier = onehot(iota((toks, toks), 1) < iota((toks, toks), 0))
    r0 = dot(earlier, o0.astype(BF))
    r1 = dot(earlier, o1.astype(BF)) + jnp.sum(o0, axis=0, keepdims=True)
    slot = jnp.concatenate([jnp.where(m0, r0, -1.0), jnp.where(m1, r1, -1.0)], axis=0).astype(BF)
    lanes = experts * 8
    spread = onehot(iota((experts, lanes), 1) >> 3 == iota((experts, lanes), 0))
    ranked = dot(slot, spread)
    j = iota((2 * toks, lanes), 1) & 7
    pick = onehot(ranked == j.astype(F32))
    late = jnp.where(ranked == (8 + (j & 1)).astype(F32), 1.0, 0.0)
    tail = back_ref[:, :, 2048:2560].astype(F32).reshape(lanes, 512).astype(BF)
    p0, p1 = p_ref[:, 0:1], p_ref[:, 1:2]
    for q in range(4):
        cols = slice(q * 512, (q + 1) * 512)
        body = back_ref[:, :, cols].astype(F32).reshape(lanes, 512).astype(BF)
        rows = dot(pick, body) + dot(jnp.where(j >> 1 == q, late, 0.0).astype(BF), tail)
        out_ref[:, cols] = (p0 * rows[:toks] + p1 * rows[toks:]).astype(BF)


def params(mib):
    return pltpu.CompilerParams(vmem_limit_bytes=mib * 1024 * 1024)


def cost(flops, size):
    return pl.CostEstimate(flops=flops, bytes_accessed=size, transcendentals=0)


def ring(own, n_dp):
    swap = [(d, d ^ 1) for d in range(n_dp)]
    on = [(d, (d + 2 if d % 2 == 0 else d - 2) % n_dp) for d in range(n_dp)]
    pieces = [own, lax.ppermute(own, "dp", swap)]
    first, second = pieces
    for step in range(n_dp // 4 - 1):
        first, second = lax.ppermute(first, "dp", on), lax.ppermute(second, "dp", on)
        pieces += [first, second, lax.ppermute(first, "dp", swap), lax.ppermute(second, "dp", swap)]
    first = lax.ppermute(first, "dp", on)
    return pieces + [first, lax.ppermute(first, "dp", swap)]


def shards(tokens, grad_out, route_ids, route_probs, gate_up, w_down):
    toks, features = tokens.shape
    experts = lax.axis_size("expert")
    n_dp = lax.axis_size("dp")
    ids = route_ids.T
    vmem, hbm = pl.BlockSpec(memory_space=pltpu.VMEM), pl.BlockSpec(memory_space=pl.ANY)
    send = pl.pallas_call(
        pack_kernel,
        in_specs=[hbm, hbm, hbm],
        out_specs=hbm,
        out_shape=jax.ShapeDtypeStruct((experts, 16, 2560), BF),
        scratch_shapes=[
            pltpu.VMEM(ids.shape, I32),
            pltpu.VMEM((toks, features), BF),
            pltpu.VMEM((toks, features), BF),
            pltpu.VMEM((experts, 16, 2560), BF),
            pltpu.SemaphoreType.DMA((3,)),
            pltpu.SemaphoreType.DMA((5,)),
        ],
        compiler_params=params(60),
        cost_estimate=cost(10**9, 4000000),
        name="pack_rows",
    )(ids, tokens, grad_out)
    rows = lax.all_to_all(send, "expert", split_axis=0, concat_axis=0, tiled=True)
    own_w = pl.pallas_call(
        weights_kernel,
        out_shape=jax.ShapeDtypeStruct((3, 128, 768), BF),
        compiler_params=params(20),
        cost_estimate=cost(10**8, 1200000),
        name="join_weights",
    )(gate_up, w_down)
    pieces = ring(own_w, n_dp)
    back = pl.pallas_call(
        expert_kernel,
        in_specs=[hbm] * (1 + len(pieces)),
        out_specs=hbm,
        out_shape=jax.ShapeDtypeStruct((experts, 8, 2688), BF),
        scratch_shapes=[
            pltpu.VMEM((experts, 16, 2560), BF),
            pltpu.VMEM((n_dp, 3, 128, 768), BF),
            pltpu.VMEM((experts * 10, features), BF),
            pltpu.VMEM((experts * 10, features), BF),
            pltpu.VMEM((experts * 10, 768), BF),
            pltpu.VMEM((experts * 10, 768), BF),
            pltpu.VMEM((experts, 8, 2688), BF),
            pltpu.SemaphoreType.DMA((5,)),
            pltpu.SemaphoreType.DMA((3, n_dp)),
            pltpu.SemaphoreType.DMA((6,)),
        ],
        compiler_params=params(60),
        cost_estimate=cost(6 * 10**9, 14000000),
        name="expert_rows",
    )(rows, *pieces)
    back = lax.all_to_all(back, "expert", split_axis=0, concat_axis=0, tiled=True)
    input_grad, prob_grad = pl.pallas_call(
        combine_kernel,
        out_shape=(jax.ShapeDtypeStruct((toks, features), BF), jax.ShapeDtypeStruct((2, toks), BF)),
        compiler_params=params(20),
        cost_estimate=cost(2 * 10**9, 2000000),
        name="combine_rows",
    )(ids, route_ids, route_probs, back)
    return input_grad, prob_grad.T


def solution(mesh):
    return jax.shard_map(
        shards,
        mesh=mesh,
        in_specs=(
            P(("dp", "expert"), None),
            P(("dp", "expert"), None),
            P(("dp", "expert"), None),
            P(("dp", "expert"), None),
            P("expert", None, "dp", None),
            P("expert", None, "dp"),
        ),
        out_specs=(P(("dp", "expert"), None), P(("dp", "expert"), None)),
        check_vma=False,
    )
```

```python
import jax
import jax.numpy as jnp
from jax import lax
from jax.experimental import pallas as pl
from jax.experimental.pallas import tpu as pltpu
from jax.sharding import PartitionSpec as P

BF = jnp.bfloat16
F32 = jnp.float32
I32 = jnp.int32


def iota(shape, dim):
    return lax.broadcasted_iota(I32, shape, dim)


def dot(a, b):
    return jnp.dot(a, b, preferred_element_type=F32)


def dot_nt(a, b):
    return lax.dot_general(a, b, (((1,), (1,)), ((), ())), preferred_element_type=F32)


def onehot(cond):
    return jnp.where(cond, 1.0, 0.0).astype(BF)


def ranks(ids, experts):
    toks = ids.shape[1]
    e = iota((experts, toks), 0)
    m0, m1 = e == ids[0:1, :], e == ids[1:2, :]
    o0, o1 = jnp.where(m0, 1.0, 0.0), jnp.where(m1, 1.0, 0.0)
    earlier = onehot(iota((toks, toks), 0) < iota((toks, toks), 1))
    r0 = dot(o0.astype(BF), earlier)
    r1 = dot(o1.astype(BF), earlier) + jnp.sum(o0, axis=1, keepdims=True)
    return jnp.where(m0, r0, -1.0), jnp.where(m1, r1, -1.0)


def weights_kernel(gu_ref, wd_ref, out_ref):
    out_ref[0:2] = gu_ref[0]
    eye = onehot(iota((128, 128), 0) == iota((128, 128), 1))
    out_ref[2] = dot_nt(eye, wd_ref[0]).astype(BF)


def quarters(x):
    return jnp.concatenate([x[:, q * 512 : (q + 1) * 512] for q in range(4)], axis=0)


def stream(src, dst, sem, columns):
    return [
        pltpu.make_async_copy(src.at[:, :, pl.ds(at, size)], dst.at[:, :, pl.ds(at, size)], sem)
        for at, size in columns
    ]


def pack_kernel(ids_hbm, tok_hbm, grad_hbm, out_hbm, ids_ref, tok_ref, grad_ref, out_ref, sems, out_sem):
    refs = (tok_ref, grad_ref)
    ids_load = pltpu.make_async_copy(ids_hbm, ids_ref, sems.at[2])
    ids_load.start()
    loads = [pltpu.make_async_copy(src, to, sems.at[i]) for i, (src, to) in enumerate(zip((tok_hbm, grad_hbm), refs))]
    for load in loads:
        load.start()
    experts = out_ref.shape[0]
    toks = tok_ref.shape[0]
    ids_load.wait()
    k0, k1 = ranks(ids_ref[...], experts)
    slot = jnp.maximum(k0, k1).astype(BF)
    rows = experts * 8
    spread = onehot(iota((rows, experts), 0) >> 3 == iota((rows, experts), 1))
    ranked = dot(spread, slot)
    row = iota((rows, toks), 0)
    pick = onehot(ranked == (row & 7).astype(F32))
    late = jnp.where(ranked == (8 + (row & 1)).astype(F32), 1.0, 0.0)
    picks = jnp.concatenate([jnp.where((row & 7) >> 1 == q, late, 0.0).astype(BF) for q in range(4)], axis=1)
    for load in loads:
        load.wait()
    stores = stream(out_ref, out_hbm, out_sem, [(c * 512, 512) for c in range(5)])
    for c in range(4):
        cols = slice(c * 512, (c + 1) * 512)
        parts = [dot(pick, ref[:, cols]).reshape(experts, 8, 512) for ref in refs]
        out_ref[:, :, cols] = jnp.concatenate(parts, axis=1).astype(BF)
        stores[c].start()
    parts = [dot(picks, quarters(ref[...])).reshape(experts, 8, 512) for ref in refs]
    out_ref[:, :, 2048:2560] = jnp.concatenate(parts, axis=1).astype(BF)
    stores[4].start()
    pltpu.make_async_copy(out_ref, out_hbm, out_sem).wait()


def owners(dp, n_dp):
    chips, chip, core = n_dp // 2, dp >> 1, dp & 1
    out = []
    for hops in range(chips // 2 + 1):
        up, down = (chip + hops) % chips, (chip + chips - hops) % chips
        here = (down * (1 - core) + up * core) * 2
        there = (up * (1 - core) + down * core) * 2
        out += [here + core, here + 1 - core, there + 1 - core, there + core]
    return out[:2] + out[4:-4] + [out[-4], out[-2]]


def expert_kernel(x_hbm, *refs):
    pieces, (out_hbm, x_ref, w, xs, gs, gg, ug, out_ref, x_sems, sems, out_sem) = refs[:-11], refs[-11:]
    sources = x_ref.shape[0]
    main, extra = sources * 8, sources * 2
    places = owners(lax.axis_index("dp"), len(pieces))
    loads = [pltpu.make_async_copy(x_hbm.at[:, :, pl.ds(c * 512, 512)], x_ref.at[:, :, pl.ds(c * 512, 512)], x_sems.at[c]) for c in range(5)]
    for load in loads:
        load.start()
    copies = []
    for n in range(3):
        cols = pl.ds(n * 256, 256)
        copies.append(
            [
                pltpu.make_async_copy(src.at[:, :, cols], w.at[at, :, :, cols], sems.at[n])
                for src, at in zip(pieces, places, strict=True)
            ]
        )
    for c in copies[0]:
        c.start()
    stores = stream(out_ref, out_hbm, out_sem, [(q * 512, 512) for q in range(5)] + [(2560, 128)])
    for c in range(4):
        loads[c].wait()
        cols = slice(c * 512, (c + 1) * 512)
        both = x_ref[:, :, cols].astype(F32)
        xs[0:main, cols] = both[:, :8].reshape(main, 512).astype(BF)
        gs[0:main, cols] = both[:, 8:].reshape(main, 512).astype(BF)
    for c in copies[1]:
        c.start()
    loads[4].wait()
    both = x_ref[:, :, 2048:2560].astype(F32)
    dst, src = iota((main, main), 0), iota((main, main), 1)
    gather = onehot(src == ((dst % extra) >> 1) * 8 + (dst // extra) * 2 + (dst & 1))
    for to, half in ((xs, both[:, :8]), (gs, both[:, 8:])):
        tail = dot(gather, half.reshape(main, 512).astype(BF)).astype(BF)
        for q in range(4):
            to[main : main + extra, q * 512 : (q + 1) * 512] = tail[q * extra : (q + 1) * extra]
    prob = jnp.zeros((main + extra, 1), F32)
    for n in range(3):
        third = w.at[:, :, :, pl.ds(n * 256, 256)]
        pltpu.make_async_copy(third, third, sems.at[n]).wait()
        if n == 0:
            for c in copies[2]:
                c.start()
        cols = slice(n * 256, (n + 1) * 256)
        gate_pre = dot(xs[...], w[:, 0, :, cols].reshape(2048, 256))
        up_value = dot(xs[...], w[:, 1, :, cols].reshape(2048, 256))
        hidden_grad = dot(gs[...], w[:, 2, :, cols].reshape(2048, 256))
        sig = jax.nn.sigmoid(gate_pre)
        act = gate_pre * sig
        hidden = (act * up_value).astype(BF).astype(F32)
        prob = prob + jnp.sum(hidden * hidden_grad, axis=1, keepdims=True)
        gg[:, cols] = (hidden_grad * up_value * sig * (1.0 + gate_pre * (1.0 - sig))).astype(BF)
        ug[:, cols] = (hidden_grad * act).astype(BF)
    rows = main + extra
    row, lane = iota((rows, 128), 0), iota((rows, 128), 1)
    slot = jnp.where(row < main, row & 7, 8 + (row & 1))
    placed = jnp.where(lane == slot, jnp.broadcast_to(prob, (rows, 128)), 0.0).astype(BF)
    at, row = iota((main, rows), 0), iota((main, rows), 1)
    source = jnp.where(row < main, row >> 3, (row - main) >> 1)
    placed = dot(onehot(at == source * 8), placed).reshape(sources, 8, 128)
    out_ref[:, :, 2560:2688] = placed.astype(BF)
    stores[5].start()
    tails = []
    for q in range(4):
        feats = slice(q * 4, (q + 1) * 4)
        row_grad = dot_nt(gg[...], w[feats, 0].reshape(512, 768)) + dot_nt(ug[...], w[feats, 1].reshape(512, 768))
        tails.append(row_grad[main:].astype(BF))
        out_ref[:, :, q * 512 : (q + 1) * 512] = row_grad[:main].reshape(sources, 8, 512).astype(BF)
        stores[q].start()
    tail = jnp.concatenate(tails, axis=0)
    scatter = onehot(src == ((dst >> 1) & 3) * extra + (dst >> 3) * 2 + (dst & 1))
    out_ref[:, :, 2048:2560] = dot(scatter, tail).reshape(sources, 8, 512).astype(BF)
    stores[4].start()
    pltpu.make_async_copy(out_ref, out_hbm, out_sem).wait()


def combine_kernel(ids_ref, ids_t_ref, p_ref, back_ref, out_ref, prob_out_ref):
    experts = back_ref.shape[0]
    toks = p_ref.shape[0]
    k0, k1 = ranks(ids_ref[...], experts)
    prob = back_ref[:, :, 2560:2688].astype(F32)[:, 0]
    for k, slots in enumerate((k0, k1)):
        acc = jnp.zeros((experts, toks), F32)
        for r in range(10):
            acc = acc + jnp.where(slots == r, jnp.broadcast_to(prob[:, r : r + 1], (experts, toks)), 0.0)
        prob_out_ref[k : k + 1, :] = jnp.sum(acc, axis=0, keepdims=True).astype(BF)
    ids_t = ids_t_ref[...]
    e = iota((toks, experts), 1)
    m0, m1 = e == ids_t[:, 0:1], e == ids_t[:, 1:2]
    o0, o1 = jnp.where(m0, 1.0, 0.0), jnp.where(m1, 1.0, 0.0)
    earlier = onehot(iota((toks, toks), 1) < iota((toks, toks), 0))
    r0 = dot(earlier, o0.astype(BF))
    r1 = dot(earlier, o1.astype(BF)) + jnp.sum(o0, axis=0, keepdims=True)
    slot = jnp.concatenate([jnp.where(m0, r0, -1.0), jnp.where(m1, r1, -1.0)], axis=0).astype(BF)
    lanes = experts * 8
    spread = onehot(iota((experts, lanes), 1) >> 3 == iota((experts, lanes), 0))
    ranked = dot(slot, spread)
    j = iota((2 * toks, lanes), 1) & 7
    pick = onehot(ranked == j.astype(F32))
    late = jnp.where(ranked == (8 + (j & 1)).astype(F32), 1.0, 0.0)
    tail = back_ref[:, :, 2048:2560].astype(F32).reshape(lanes, 512).astype(BF)
    p0, p1 = p_ref[:, 0:1], p_ref[:, 1:2]
    for q in range(4):
        cols = slice(q * 512, (q + 1) * 512)
        body = back_ref[:, :, cols].astype(F32).reshape(lanes, 512).astype(BF)
        rows = dot(pick, body) + dot(jnp.where(j >> 1 == q, late, 0.0).astype(BF), tail)
        out_ref[:, cols] = (p0 * rows[:toks] + p1 * rows[toks:]).astype(BF)


def params(mib):
    return pltpu.CompilerParams(vmem_limit_bytes=mib * 1024 * 1024)


def cost(flops, size):
    return pl.CostEstimate(flops=flops, bytes_accessed=size, transcendentals=0)


def ring(own, n_dp):
    swap = [(d, d ^ 1) for d in range(n_dp)]
    on = [(d, (d + 2 if d % 2 == 0 else d - 2) % n_dp) for d in range(n_dp)]
    pieces = [own, lax.ppermute(own, "dp", swap)]
    first, second = pieces
    for step in range(n_dp // 4 - 1):
        first, second = lax.ppermute(first, "dp", on), lax.ppermute(second, "dp", on)
        pieces += [first, second, lax.ppermute(first, "dp", swap), lax.ppermute(second, "dp", swap)]
    first = lax.ppermute(first, "dp", on)
    return pieces + [first, lax.ppermute(first, "dp", swap)]


def shards(tokens, grad_out, route_ids, route_probs, gate_up, w_down):
    toks, features = tokens.shape
    experts = lax.axis_size("expert")
    n_dp = lax.axis_size("dp")
    ids = route_ids.T
    vmem, hbm = pl.BlockSpec(memory_space=pltpu.VMEM), pl.BlockSpec(memory_space=pl.ANY)
    send = pl.pallas_call(
        pack_kernel,
        in_specs=[hbm, hbm, hbm],
        out_specs=hbm,
        out_shape=jax.ShapeDtypeStruct((experts, 16, 2560), BF),
        scratch_shapes=[
            pltpu.VMEM(ids.shape, I32),
            pltpu.VMEM((toks, features), BF),
            pltpu.VMEM((toks, features), BF),
            pltpu.VMEM((experts, 16, 2560), BF),
            pltpu.SemaphoreType.DMA((3,)),
            pltpu.SemaphoreType.DMA,
        ],
        compiler_params=params(60),
        cost_estimate=cost(10**9, 4000000),
        name="pack_rows",
    )(ids, tokens, grad_out)
    rows = lax.all_to_all(send, "expert", split_axis=0, concat_axis=0, tiled=True)
    own_w = pl.pallas_call(
        weights_kernel,
        out_shape=jax.ShapeDtypeStruct((3, 128, 768), BF),
        compiler_params=params(20),
        cost_estimate=cost(10**8, 1200000),
        name="join_weights",
    )(gate_up, w_down)
    pieces = ring(own_w, n_dp)
    back = pl.pallas_call(
        expert_kernel,
        in_specs=[hbm] * (1 + len(pieces)),
        out_specs=hbm,
        out_shape=jax.ShapeDtypeStruct((experts, 8, 2688), BF),
        scratch_shapes=[
            pltpu.VMEM((experts, 16, 2560), BF),
            pltpu.VMEM((n_dp, 3, 128, 768), BF),
            pltpu.VMEM((experts * 10, features), BF),
            pltpu.VMEM((experts * 10, features), BF),
            pltpu.VMEM((experts * 10, 768), BF),
            pltpu.VMEM((experts * 10, 768), BF),
            pltpu.VMEM((experts, 8, 2688), BF),
            pltpu.SemaphoreType.DMA((5,)),
            pltpu.SemaphoreType.DMA((3,)),
            pltpu.SemaphoreType.DMA,
        ],
        compiler_params=params(60),
        cost_estimate=cost(6 * 10**9, 14000000),
        name="expert_rows",
    )(rows, *pieces)
    back = lax.all_to_all(back, "expert", split_axis=0, concat_axis=0, tiled=True)
    input_grad, prob_grad = pl.pallas_call(
        combine_kernel,
        out_shape=(jax.ShapeDtypeStruct((toks, features), BF), jax.ShapeDtypeStruct((2, toks), BF)),
        compiler_params=params(20),
        cost_estimate=cost(2 * 10**9, 2000000),
        name="combine_rows",
    )(ids, route_ids, route_probs, back)
    return input_grad, prob_grad.T


def solution(mesh):
    return jax.shard_map(
        shards,
        mesh=mesh,
        in_specs=(
            P(("dp", "expert"), None),
            P(("dp", "expert"), None),
            P(("dp", "expert"), None),
            P(("dp", "expert"), None),
            P("expert", None, "dp", None),
            P("expert", None, "dp"),
        ),
        out_specs=(P(("dp", "expert"), None), P(("dp", "expert"), None)),
        check_vma=False,
    )
```

```python
import jax
import jax.numpy as jnp
from jax import lax
from jax.experimental import pallas as pl
from jax.experimental.pallas import tpu as pltpu
from jax.sharding import PartitionSpec as P

BF = jnp.bfloat16
F32 = jnp.float32
I32 = jnp.int32


def iota(shape, dim):
    return lax.broadcasted_iota(I32, shape, dim)


def dot(a, b):
    return jnp.dot(a, b, preferred_element_type=F32)


def dot_nt(a, b):
    return lax.dot_general(a, b, (((1,), (1,)), ((), ())), preferred_element_type=F32)


def onehot(cond):
    return jnp.where(cond, 1.0, 0.0).astype(BF)


def ranks(ids, experts):
    toks = ids.shape[1]
    e = iota((experts, toks), 0)
    m0, m1 = e == ids[0:1, :], e == ids[1:2, :]
    o0, o1 = jnp.where(m0, 1.0, 0.0), jnp.where(m1, 1.0, 0.0)
    earlier = onehot(iota((toks, toks), 0) < iota((toks, toks), 1))
    r0 = dot(o0.astype(BF), earlier)
    r1 = dot(o1.astype(BF), earlier) + jnp.sum(o0, axis=1, keepdims=True)
    return jnp.where(m0, r0, -1.0), jnp.where(m1, r1, -1.0)


def weights_kernel(gu_ref, wd_ref, out_ref):
    out_ref[0:2] = gu_ref[0]
    eye = onehot(iota((128, 128), 0) == iota((128, 128), 1))
    out_ref[2] = dot_nt(eye, wd_ref[0]).astype(BF)


def quarters(x):
    return jnp.concatenate([x[:, q * 512 : (q + 1) * 512] for q in range(4)], axis=0)


def stream(src, dst, sem, columns):
    return [
        pltpu.make_async_copy(src.at[:, :, pl.ds(at, size)], dst.at[:, :, pl.ds(at, size)], sem)
        for at, size in columns
    ]


def pack_kernel(ids_hbm, tok_hbm, grad_hbm, out_hbm, ids_ref, tok_ref, grad_ref, out_ref, sems, out_sem):
    refs = (tok_ref, grad_ref)
    ids_load = pltpu.make_async_copy(ids_hbm, ids_ref, sems.at[2])
    ids_load.start()
    loads = [pltpu.make_async_copy(src, to, sems.at[i]) for i, (src, to) in enumerate(zip((tok_hbm, grad_hbm), refs))]
    for load in loads:
        load.start()
    experts = out_ref.shape[0]
    toks = tok_ref.shape[0]
    ids_load.wait()
    k0, k1 = ranks(ids_ref[...], experts)
    slot = jnp.maximum(k0, k1).astype(BF)
    rows = experts * 8
    spread = onehot(iota((rows, experts), 0) >> 3 == iota((rows, experts), 1))
    ranked = dot(spread, slot)
    row = iota((rows, toks), 0)
    pick = onehot(ranked == (row & 7).astype(F32))
    late = jnp.where(ranked == (8 + (row & 1)).astype(F32), 1.0, 0.0)
    picks = jnp.concatenate([jnp.where((row & 7) >> 1 == q, late, 0.0).astype(BF) for q in range(4)], axis=1)
    for load in loads:
        load.wait()
    stores = stream(out_ref, out_hbm, out_sem, [(c * 512, 512) for c in range(5)])
    for c in range(4):
        cols = slice(c * 512, (c + 1) * 512)
        parts = [dot(pick, ref[:, cols]).reshape(experts, 8, 512) for ref in refs]
        out_ref[:, :, cols] = jnp.concatenate(parts, axis=1).astype(BF)
        stores[c].start()
    parts = [dot(picks, quarters(ref[...])).reshape(experts, 8, 512) for ref in refs]
    out_ref[:, :, 2048:2560] = jnp.concatenate(parts, axis=1).astype(BF)
    stores[4].start()
    pltpu.make_async_copy(out_ref, out_hbm, out_sem).wait()


def owners(dp, n_dp):
    chips, chip, core = n_dp // 2, dp >> 1, dp & 1
    out = []
    for hops in range(chips // 2 + 1):
        up, down = (chip + hops) % chips, (chip + chips - hops) % chips
        here = (down * (1 - core) + up * core) * 2
        there = (up * (1 - core) + down * core) * 2
        out += [here + core, here + 1 - core, there + 1 - core, there + core]
    return out[:2] + out[4:-4] + [out[-4], out[-2]]


def expert_kernel(x_hbm, *refs):
    pieces, (out_hbm, x_ref, w, xs, gs, gg, ug, out_ref, x_sems, sems, out_sem) = refs[:-11], refs[-11:]
    sources = x_ref.shape[0]
    main, extra = sources * 8, sources * 2
    places = owners(lax.axis_index("dp"), len(pieces))
    loads = [pltpu.make_async_copy(x_hbm.at[:, :, pl.ds(c * 512, 512)], x_ref.at[:, :, pl.ds(c * 512, 512)], x_sems.at[c]) for c in range(5)]
    for load in loads:
        load.start()
    copies = []
    for n in range(3):
        cols = pl.ds(n * 256, 256)
        copies.append(
            [
                pltpu.make_async_copy(src.at[:, :, cols], w.at[at, :, :, cols], sems.at[n])
                for src, at in zip(pieces, places, strict=True)
            ]
        )
    for c in copies[0]:
        c.start()
    stores = stream(out_ref, out_hbm, out_sem, [(q * 512, 512) for q in range(5)] + [(2560, 128)])
    for c in range(4):
        loads[c].wait()
        cols = slice(c * 512, (c + 1) * 512)
        both = x_ref[:, :, cols].astype(F32)
        xs[0:main, cols] = both[:, :8].reshape(main, 512).astype(BF)
        gs[0:main, cols] = both[:, 8:].reshape(main, 512).astype(BF)
    for c in copies[1]:
        c.start()
    loads[4].wait()
    both = x_ref[:, :, 2048:2560].astype(F32)
    dst, src = iota((main, main), 0), iota((main, main), 1)
    gather = onehot(src == ((dst % extra) >> 1) * 8 + (dst // extra) * 2 + (dst & 1))
    for to, half in ((xs, both[:, :8]), (gs, both[:, 8:])):
        tail = dot(gather, half.reshape(main, 512).astype(BF)).astype(BF)
        for q in range(4):
            to[main : main + extra, q * 512 : (q + 1) * 512] = tail[q * extra : (q + 1) * extra]
    prob = jnp.zeros((main + extra, 1), F32)
    for n in range(3):
        third = w.at[:, :, :, pl.ds(n * 256, 256)]
        pltpu.make_async_copy(third, third, sems.at[n]).wait()
        if n == 0:
            for c in copies[2]:
                c.start()
        cols = slice(n * 256, (n + 1) * 256)
        gate_pre = dot(xs[...], w[:, 0, :, cols].reshape(2048, 256))
        up_value = dot(xs[...], w[:, 1, :, cols].reshape(2048, 256))
        hidden_grad = dot(gs[...], w[:, 2, :, cols].reshape(2048, 256))
        sig = jax.nn.sigmoid(gate_pre)
        act = gate_pre * sig
        hidden = (act * up_value).astype(BF).astype(F32)
        prob = prob + jnp.sum(hidden * hidden_grad, axis=1, keepdims=True)
        gg[:, cols] = (hidden_grad * up_value * sig * (1.0 + gate_pre * (1.0 - sig))).astype(BF)
        ug[:, cols] = (hidden_grad * act).astype(BF)
    rows = main + extra
    row, lane = iota((rows, 128), 0), iota((rows, 128), 1)
    slot = jnp.where(row < main, row & 7, 8 + (row & 1))
    placed = jnp.where(lane == slot, jnp.broadcast_to(prob, (rows, 128)), 0.0).astype(BF)
    at, row = iota((main, rows), 0), iota((main, rows), 1)
    source = jnp.where(row < main, row >> 3, (row - main) >> 1)
    placed = dot(onehot(at == source * 8), placed).reshape(sources, 8, 128)
    out_ref[:, :, 2560:2688] = placed.astype(BF)
    stores[5].start()
    tails = []
    for q in range(4):
        feats = slice(q * 4, (q + 1) * 4)
        row_grad = dot_nt(gg[...], w[feats, 0].reshape(512, 768)) + dot_nt(ug[...], w[feats, 1].reshape(512, 768))
        tails.append(row_grad[main:].astype(BF))
        out_ref[:, :, q * 512 : (q + 1) * 512] = row_grad[:main].reshape(sources, 8, 512).astype(BF)
        stores[q].start()
    tail = jnp.concatenate(tails, axis=0)
    scatter = onehot(src == ((dst >> 1) & 3) * extra + (dst >> 3) * 2 + (dst & 1))
    out_ref[:, :, 2048:2560] = dot(scatter, tail).reshape(sources, 8, 512).astype(BF)
    stores[4].start()
    pltpu.make_async_copy(out_ref, out_hbm, out_sem).wait()


def combine_kernel(ids_ref, ids_t_ref, p_ref, back_ref, out_hbm, prob_out_ref, out_ref, out_sem):
    experts = back_ref.shape[0]
    toks = p_ref.shape[0]
    k0, k1 = ranks(ids_ref[...], experts)
    prob = back_ref[:, :, 2560:2688].astype(F32)[:, 0]
    for k, slots in enumerate((k0, k1)):
        acc = jnp.zeros((experts, toks), F32)
        for r in range(10):
            acc = acc + jnp.where(slots == r, jnp.broadcast_to(prob[:, r : r + 1], (experts, toks)), 0.0)
        prob_out_ref[k : k + 1, :] = jnp.sum(acc, axis=0, keepdims=True).astype(BF)
    ids_t = ids_t_ref[...]
    e = iota((toks, experts), 1)
    m0, m1 = e == ids_t[:, 0:1], e == ids_t[:, 1:2]
    o0, o1 = jnp.where(m0, 1.0, 0.0), jnp.where(m1, 1.0, 0.0)
    earlier = onehot(iota((toks, toks), 1) < iota((toks, toks), 0))
    r0 = dot(earlier, o0.astype(BF))
    r1 = dot(earlier, o1.astype(BF)) + jnp.sum(o0, axis=0, keepdims=True)
    slot = jnp.concatenate([jnp.where(m0, r0, -1.0), jnp.where(m1, r1, -1.0)], axis=0).astype(BF)
    lanes = experts * 8
    spread = onehot(iota((experts, lanes), 1) >> 3 == iota((experts, lanes), 0))
    ranked = dot(slot, spread)
    j = iota((2 * toks, lanes), 1) & 7
    pick = onehot(ranked == j.astype(F32))
    late = jnp.where(ranked == (8 + (j & 1)).astype(F32), 1.0, 0.0)
    tail = back_ref[:, :, 2048:2560].astype(F32).reshape(lanes, 512).astype(BF)
    p0, p1 = p_ref[:, 0:1], p_ref[:, 1:2]
    for q in range(4):
        cols = slice(q * 512, (q + 1) * 512)
        body = back_ref[:, :, cols].astype(F32).reshape(lanes, 512).astype(BF)
        rows = dot(pick, body) + dot(jnp.where(j >> 1 == q, late, 0.0).astype(BF), tail)
        out_ref[:, cols] = (p0 * rows[:toks] + p1 * rows[toks:]).astype(BF)
        part = pl.ds(q * 512, 512)
        pltpu.make_async_copy(out_ref.at[:, part], out_hbm.at[:, part], out_sem).start()
    pltpu.make_async_copy(out_ref, out_hbm, out_sem).wait()


def params(mib):
    return pltpu.CompilerParams(vmem_limit_bytes=mib * 1024 * 1024)


def cost(flops, size):
    return pl.CostEstimate(flops=flops, bytes_accessed=size, transcendentals=0)


def ring(own, n_dp):
    swap = [(d, d ^ 1) for d in range(n_dp)]
    on = [(d, (d + 2 if d % 2 == 0 else d - 2) % n_dp) for d in range(n_dp)]
    pieces = [own, lax.ppermute(own, "dp", swap)]
    first, second = pieces
    for step in range(n_dp // 4 - 1):
        first, second = lax.ppermute(first, "dp", on), lax.ppermute(second, "dp", on)
        pieces += [first, second, lax.ppermute(first, "dp", swap), lax.ppermute(second, "dp", swap)]
    first = lax.ppermute(first, "dp", on)
    return pieces + [first, lax.ppermute(first, "dp", swap)]


def shards(tokens, grad_out, route_ids, route_probs, gate_up, w_down):
    toks, features = tokens.shape
    experts = lax.axis_size("expert")
    n_dp = lax.axis_size("dp")
    ids = route_ids.T
    vmem, hbm = pl.BlockSpec(memory_space=pltpu.VMEM), pl.BlockSpec(memory_space=pl.ANY)
    send = pl.pallas_call(
        pack_kernel,
        in_specs=[hbm, hbm, hbm],
        out_specs=hbm,
        out_shape=jax.ShapeDtypeStruct((experts, 16, 2560), BF),
        scratch_shapes=[
            pltpu.VMEM(ids.shape, I32),
            pltpu.VMEM((toks, features), BF),
            pltpu.VMEM((toks, features), BF),
            pltpu.VMEM((experts, 16, 2560), BF),
            pltpu.SemaphoreType.DMA((3,)),
            pltpu.SemaphoreType.DMA,
        ],
        compiler_params=params(60),
        cost_estimate=cost(10**9, 4000000),
        name="pack_rows",
    )(ids, tokens, grad_out)
    rows = lax.all_to_all(send, "expert", split_axis=0, concat_axis=0, tiled=True)
    own_w = pl.pallas_call(
        weights_kernel,
        out_shape=jax.ShapeDtypeStruct((3, 128, 768), BF),
        compiler_params=params(20),
        cost_estimate=cost(10**8, 1200000),
        name="join_weights",
    )(gate_up, w_down)
    pieces = ring(own_w, n_dp)
    back = pl.pallas_call(
        expert_kernel,
        in_specs=[hbm] * (1 + len(pieces)),
        out_specs=hbm,
        out_shape=jax.ShapeDtypeStruct((experts, 8, 2688), BF),
        scratch_shapes=[
            pltpu.VMEM((experts, 16, 2560), BF),
            pltpu.VMEM((n_dp, 3, 128, 768), BF),
            pltpu.VMEM((experts * 10, features), BF),
            pltpu.VMEM((experts * 10, features), BF),
            pltpu.VMEM((experts * 10, 768), BF),
            pltpu.VMEM((experts * 10, 768), BF),
            pltpu.VMEM((experts, 8, 2688), BF),
            pltpu.SemaphoreType.DMA((5,)),
            pltpu.SemaphoreType.DMA((3,)),
            pltpu.SemaphoreType.DMA,
        ],
        compiler_params=params(60),
        cost_estimate=cost(6 * 10**9, 14000000),
        name="expert_rows",
    )(rows, *pieces)
    back = lax.all_to_all(back, "expert", split_axis=0, concat_axis=0, tiled=True)
    input_grad, prob_grad = pl.pallas_call(
        combine_kernel,
        out_specs=(hbm, vmem),
        out_shape=(jax.ShapeDtypeStruct((toks, features), BF), jax.ShapeDtypeStruct((2, toks), BF)),
        scratch_shapes=[pltpu.VMEM((toks, features), BF), pltpu.SemaphoreType.DMA],
        compiler_params=params(20),
        cost_estimate=cost(2 * 10**9, 2000000),
        name="combine_rows",
    )(ids, route_ids, route_probs, back)
    return input_grad, prob_grad.T


def solution(mesh):
    return jax.shard_map(
        shards,
        mesh=mesh,
        in_specs=(
            P(("dp", "expert"), None),
            P(("dp", "expert"), None),
            P(("dp", "expert"), None),
            P(("dp", "expert"), None),
            P("expert", None, "dp", None),
            P("expert", None, "dp"),
        ),
        out_specs=(P(("dp", "expert"), None), P(("dp", "expert"), None)),
        check_vma=False,
    )
```
